512 devices in a mesh: req: 32 (over z, core), seq: 16 (over x, y).
Axes of the slice: x: 4, y: 4, z: 16, core: 2. Of those that a mesh axis runs over, the one named last changes fastest.
Arguments:
- queries: bfloat16 [32768, 2560], P(('req', 'seq')), parts along dimension 0, may hold values from -30 to 30
- keys: bfloat16 [131072, 2560], P(('req', 'seq')), parts along dimension 0, may hold values from -30 to 30
- values: bfloat16 [131072, 2560], P(('req', 'seq')), parts along dimension 0, may hold values from -6 to 6
- active_blocks: int32 [256], P('req'), parts along dimension 0, may hold values from 0 to 31, as said below
Outputs:
- edited: bfloat16 [131072, 2560], P(('req', 'seq')), parts along dimension 0
The draws below stay inside these ranges and needn't reach their ends.
There are 32 independent parts, one for each index of `req`. The reference program is written for one: setup_inputs(seed, part) draws one part's arguments, and reference() takes and returns one part's arrays. A program takes and returns all parts, laid end to end along the dimension named above; each array names one. Nothing has to cross between parts.
Inputs may be any that keep to these rules, and one draw needn't show every extreme that they name: `active_blocks`: distinct block numbers; block b holds tokens b * 128 to b * 128 + 127.
All inputs are finite; a program needn't handle non-finite values.
Results may differ from the reference program's by a relative error of at most 0.006.
Values may be sent and summed in bfloat16 or wider, within the bound.
A program may use at most 128 MiB of HBM per device.

```python
import jax
import jax.numpy as jnp
from jax import lax

HEADS = 20
HD = 128
BLK = 128
BPD = 2
TOK_DEV = 256
TOKENS = 4096
ACT = 8
N_SEQ = 16


def draw_queries(key, part):
    key = jax.random.fold_in(key, 21)
    total_rows = ACT * BLK
    drawn = jnp.clip(2.5 * jax.random.normal(key, (total_rows, HEADS * HD), jnp.float32), -12.0, 12.0)
    return drawn.astype(jnp.bfloat16)


def draw_keys(key, part):
    key = jax.random.fold_in(key, 37)
    drawn = jnp.clip(jax.random.normal(key, (TOKENS, HEADS * HD), jnp.float32), -6.0, 6.0)
    return drawn.astype(jnp.bfloat16)


def draw_active_blocks(key, part):
    key = jax.random.fold_in(key, 53)
    block_total = N_SEQ * BPD
    key_owner, key_rank, key_shuffle = jax.random.split(key, 3)
    owner_pick = jax.random.randint(key_owner, (), 0, N_SEQ)
    order_rank = jax.random.permutation(key_rank, block_total)
    positions = jnp.arange(block_total)
    forced = (positions // BPD == owner_pick) & (positions % BPD < 2)
    ranking = jnp.where(forced, positions % BPD - 2, order_rank)
    ranking = jnp.where(positions == block_total - 1, -3, ranking)
    chosen = jnp.argsort(ranking, stable=True)[:ACT]
    shuffled = chosen[jax.random.permutation(key_shuffle, ACT)]
    return shuffled.astype(jnp.int32)


def block_levels(key, dims, cuts, low, high):
    factor_of, own = 1.0, jax.random.fold_in(key, 6)
    for axis_at, parts in cuts:
        steps = jnp.exp(jax.random.uniform(jax.random.fold_in(own, axis_at), (parts,), jnp.float32, low / len(cuts), high / len(cuts)))
        factor_of = factor_of * jnp.repeat(steps, dims[axis_at] // parts).reshape([-1 if axis == axis_at else 1 for axis in range(len(dims))])
    return factor_of


def bell_draw(key, shape, scale, bound, shards=(), kind=jnp.bfloat16):
    factor_of = block_levels(key, shape, shards, -0.22, 0.18) if shards else 1.0
    array = jax.random.normal(key, shape, jnp.float32) * scale * factor_of
    return jnp.minimum(jnp.maximum(array, -bound), bound).astype(kind)


def setup_inputs(seed: int = 0, part: int = 0) -> dict:
    seeds = jax.random.split(jax.random.key(seed), 5)
    part_splits = jax.random.split(jax.random.fold_in(seeds[4], part), 5)
    queries = draw_queries(jax.random.fold_in(jax.random.fold_in(seeds[4], part), 71), part)
    keys = draw_keys(jax.random.fold_in(jax.random.fold_in(seeds[4], part), 71), part)
    values = bell_draw(part_splits[2], (TOKENS, HEADS * HD), 1.0, 6.0, ((0, 16),))
    active_blocks = draw_active_blocks(jax.random.fold_in(jax.random.fold_in(seeds[4], part), 71), part)
    return {"queries": queries, "keys": keys, "values": values, "active_blocks": active_blocks}


def shard_partials(queries, key_part, value_part):
    row_count = queries.shape[0]
    key_count = key_part.shape[0]
    query_heads = queries.reshape(row_count, HEADS, HD).astype(jnp.float32)
    key_heads = key_part.reshape(key_count, HEADS, HD).astype(jnp.float32)
    value_heads = value_part.reshape(key_count, HEADS, HD).astype(jnp.float32)
    scores = jnp.einsum("rhd,thd->hrt", query_heads, key_heads) * (HD ** -0.5)
    maxima = lax.optimization_barrier(jnp.max(scores, axis=-1).astype(jnp.bfloat16))
    shifted = jnp.exp(scores - maxima.astype(jnp.float32)[:, :, None])
    totals = jnp.sum(shifted, axis=-1).astype(jnp.bfloat16)
    weights = shifted.astype(jnp.bfloat16).astype(jnp.float32)
    numerators = jnp.einsum("hrt,thd->rhd", weights, value_heads).astype(jnp.bfloat16)
    return numerators, maxima.T, totals.T


def reference(queries, keys, values, active_blocks):
    total_rows = queries.shape[0]
    width = HEADS * HD

    def one_shard(shard_index):
        start = shard_index * TOK_DEV
        key_part = lax.dynamic_slice_in_dim(keys, start, TOK_DEV, 0)
        value_part = lax.dynamic_slice_in_dim(values, start, TOK_DEV, 0)
        return shard_partials(queries, key_part, value_part)

    numerators, maxima, totals = lax.map(one_shard, jnp.arange(N_SEQ, dtype=jnp.int32))
    maxima_f = maxima.astype(jnp.float32)
    highest = jnp.max(maxima_f, axis=0)
    factors = jnp.exp(maxima_f - highest[None])
    summed = jnp.einsum("srh,srhd->rhd", factors, numerators.astype(jnp.float32))
    denominators = jnp.sum(factors * totals.astype(jnp.float32), axis=0)
    attended = (summed / denominators[:, :, None]).reshape(total_rows, width).astype(jnp.bfloat16)
    edited = jnp.zeros((N_SEQ * BPD, BLK, width), jnp.bfloat16)
    edited = edited.at[active_blocks].set(attended.reshape(ACT, BLK, width))
    return edited.reshape(TOKENS, width)
```

```python
import jax
import jax.numpy as jnp
from jax import lax
from jax.experimental import pallas as pl
from jax.experimental.pallas import tpu as pltpu
from jax.sharding import PartitionSpec as P

HEADS = 20
HD = 128
BLK = 128
BPD = 2
SIDE = 4
OWN = HEADS // SIDE
ROWS = 64
TOK = 256
CHUNK = SIDE * ROWS
TOTAL = SIDE * CHUNK
GROUP = OWN * HD
SCALE = HD ** -0.5 * 1.4426950408889634
MESH = pl.DeviceIdType.MESH
OTHERS = (1, 3, 2)


def attend_head(h, qbuf, kbuf, vbuf, obuf, lbuf, eye, top):
    columns = pl.ds(pl.multiple_of(h * HD, HD), HD)
    for part in range(SIDE):
        rows = pl.ds(part * CHUNK, CHUNK)
        scores = lax.dot_general(
            qbuf[rows, columns], kbuf[h], (((1,), (1,)), ((), ())),
            preferred_element_type=jnp.float32,
        )
        high = jnp.max(scores, axis=-1, keepdims=True)
        weights = jnp.exp2((scores - high) * SCALE).astype(jnp.bfloat16)
        summed = jnp.dot(weights, vbuf[h], preferred_element_type=jnp.float32)
        totals = summed[:, HD:]
        obuf[h, rows, :] = (summed[:, :HD] / totals).astype(jnp.bfloat16)
        logs = high * SCALE + jnp.log2(totals)
        first = jnp.sum(jnp.where(eye, logs[:BLK], 0.0), axis=0, keepdims=True)
        second = jnp.sum(jnp.where(eye, logs[BLK:], 0.0), axis=0, keepdims=True)
        lbuf[h, part] = jnp.where(top, first, second)


def merge_head(h, obuf, lbuf, orecv, lrecv, att):
    logs = [lbuf[h, 0]] + [lrecv[h, i] for i in range(SIDE - 1)]
    highest = jnp.maximum(jnp.maximum(logs[0], logs[1]), jnp.maximum(logs[2], logs[3]))
    factors = [jnp.exp2(one - highest) for one in logs]
    inverse = 1.0 / (factors[0] + factors[1] + factors[2] + factors[3])
    for half in range(2):
        rows = slice(half * BLK, (half + 1) * BLK)
        total = None
        for i in range(SIDE):
            share = factors[i] * inverse
            spread = jnp.broadcast_to(share[half : half + 1, :], (BLK, HD)).T
            piece = obuf[h, rows, :] if i == 0 else orecv[h, i - 1, rows, :]
            term = spread * piece.astype(jnp.float32)
            total = term if total is None else total + term
        att[h, rows, :] = total.astype(jnp.bfloat16)


def kernel(
    act, q, k, v, out,
    qbuf, kbuf, vbuf, obuf, lbuf, orecv, lrecv, att, stage, pick,
    qs1, qr1, qs2, qr2, ks, kr, vs, vr, os, orr, ls, lr, as_, ar, ds, dr,
):
    core = lax.axis_index("req") % 2
    here = lax.axis_index("seq")
    x, y = here // SIDE, here % SIDE
    a = x + core * (y - x)
    b = y + core * (x - y)

    def device(da, db):
        ta, tb = (a + da) % SIDE, (b + db) % SIDE
        tx, ty = ta + core * (tb - ta), tb + core * (ta - tb)
        return tx * SIDE + ty

    def remote(src, dst, send, recv, da, db):
        return pltpu.make_async_remote_copy(
            src_ref=src, dst_ref=dst, send_sem=send, recv_sem=recv,
            device_id={"seq": device(da, db)}, device_id_type=MESH,
        )

    def group_columns(da):
        return pl.ds(pl.multiple_of((a + da) % SIDE * GROUP, GROUP), GROUP)

    def head_columns(da, h):
        return pl.ds(pl.multiple_of(((a + da) % SIDE * OWN + h) * HD, HD), HD)

    def query_local():
        return pltpu.make_async_copy(q.at[:, group_columns(0)], qbuf.at[pl.ds(0, ROWS)], qs1.at[0])

    def query_first(i):
        return remote(q.at[:, group_columns(i)], qbuf.at[pl.ds(i * ROWS, ROWS)], qs1.at[i], qr1.at[i], i, 0)

    def query_second(i):
        return remote(
            qbuf.at[pl.ds(0, CHUNK)], qbuf.at[pl.ds(i * CHUNK, CHUNK)], qs2.at[i], qr2.at[i], 0, i
        )

    def key_local(h):
        return pltpu.make_async_copy(k.at[:, head_columns(0, h)], kbuf.at[h, pl.ds(0, TOK)], ks.at[h, 0])

    def value_local(h):
        return pltpu.make_async_copy(
            v.at[:, head_columns(0, h)], vbuf.at[h, pl.ds(0, TOK), pl.ds(0, HD)], vs.at[h, 0]
        )

    def key_copy(h, i):
        return remote(
            k.at[:, head_columns(i, h)], kbuf.at[h, pl.ds(i * TOK, TOK)], ks.at[h, i], kr.at[h, i], i, 0
        )

    def value_copy(h, i):
        return remote(
            v.at[:, head_columns(i, h)], vbuf.at[h, pl.ds(i * TOK, TOK), pl.ds(0, HD)],
            vs.at[h, i], vr.at[h, i], i, 0,
        )

    def partial_copy(h, i):
        return remote(
            obuf.at[h, pl.ds((SIDE - i) * CHUNK, CHUNK)], orecv.at[h, i - 1],
            os.at[h, i], orr.at[h, i], 0, i,
        )

    def log_copy(h, i):
        return remote(lbuf.at[h, SIDE - i], lrecv.at[h, i - 1], ls.at[h, i], lr.at[h, i], 0, i)

    def merged_copy(h, i):
        return remote(
            att.at[h, pl.ds(0, CHUNK)], att.at[h, pl.ds(i * CHUNK, CHUNK)],
            as_.at[h, i], ar.at[h, i], 0, i,
        )

    def finished_local(h):
        return pltpu.make_async_copy(stage.at[h, 0], out.at[:, head_columns(0, h)], ds.at[h, 0])

    def finished_copy(h, i):
        return remote(stage.at[h, i], out.at[:, head_columns(0, h)], ds.at[h, i], dr.at[h, i], i, 0)

    barrier = pltpu.get_barrier_semaphore()
    for i in OTHERS:
        for da, db in ((i, 0), (0, i)):
            pl.semaphore_signal(barrier, inc=1, device_id={"seq": device(da, db)}, device_id_type=MESH)
    pl.semaphore_wait(barrier, 2 * len(OTHERS))

    query_local().start()
    for i in OTHERS:
        query_first(i).start()

    @pl.loop(0, OWN)
    def _(h):
        key_local(h).start()
        value_local(h).start()
        for i in OTHERS:
            key_copy(h, i).start()
            value_copy(h, i).start()

    @pl.loop(0, OWN)
    def _(h):
        vbuf[h, :, HD:] = jnp.ones((TOTAL, HD), jnp.bfloat16)

    query_local().wait()
    for i in OTHERS:
        query_first(i).wait()
    for i in OTHERS:
        query_second(i).start()
    for i in OTHERS:
        query_second(i).wait()

    line = lax.broadcasted_iota(jnp.int32, (BLK, HD), 0)
    eye = line == lax.broadcasted_iota(jnp.int32, (BLK, HD), 1)
    top = lax.broadcasted_iota(jnp.int32, (8, HD), 0) == 0

    pick[SIDE * SIDE] = jnp.zeros((ROWS, HD), jnp.bfloat16)
    places = []
    for owner in range(SIDE * SIDE):
        ox, oy = owner // SIDE, owner % SIDE
        oa, ob = ox + core * (oy - ox), oy + core * (ox - oy)
        places.append((b - ob + SIDE) % SIDE * SIDE + (a - oa + SIDE) % SIDE)
    sources = []
    for i in range(SIDE):
        wanted = []
        for slot in range(BPD):
            block = device(i, 0) * BPD + slot
            spots = [jnp.int32(SIDE * SIDE)] * 2
            for j in range(SIDE * SIDE // 2):
                match = act[j] == block
                spots = [jnp.where(match, places[2 * j + half], spots[half]) for half in range(2)]
            wanted += spots
        sources.append(wanted)

    @pl.loop(0, OWN + 2)
    def _(t):
        @pl.when(t < OWN)
        def _():
            key_local(t).wait()
            value_local(t).wait()
            for i in OTHERS:
                key_copy(t, i).wait()
                value_copy(t, i).wait()
            attend_head(t, qbuf, kbuf, vbuf, obuf, lbuf, eye, top)
            for i in OTHERS:
                partial_copy(t, i).start()
                log_copy(t, i).start()

        @pl.when((t >= 1) & (t < OWN + 1))
        def _():
            h = t - 1
            for i in OTHERS:
                partial_copy(h, i).wait()
                log_copy(h, i).wait()
            merge_head(h, obuf, lbuf, orecv, lrecv, att)
            for i in OTHERS:
                merged_copy(h, i).start()

        @pl.when(t >= 2)
        def _():
            h = t - 2
            for i in OTHERS:
                merged_copy(h, i).wait()
            for spot in range(SIDE * SIDE):
                pick[spot] = att[h, pl.ds(spot * ROWS, ROWS), :]
            for i in range(SIDE):
                for piece in range(2 * BPD):
                    stage[h, i, pl.ds(piece * ROWS, ROWS), :] = pick[sources[i][piece]]
            finished_local(h).start()
            for i in OTHERS:
                finished_copy(h, i).start()

    @pl.loop(0, OWN)
    def _(h):
        finished_local(h).wait()
        for i in OTHERS:
            finished_copy(h, i).wait()


def local(queries, keys, values, active_blocks):
    sems = pltpu.SemaphoreType.DMA
    bf16 = jnp.bfloat16
    return pl.pallas_call(
        kernel,
        out_shape=jax.ShapeDtypeStruct((TOK, HEADS * HD), bf16),
        in_specs=[pl.BlockSpec(memory_space=pltpu.SMEM)] + [pl.BlockSpec(memory_space=pl.ANY)] * 3,
        out_specs=pl.BlockSpec(memory_space=pl.ANY),
        scratch_shapes=[
            pltpu.VMEM((TOTAL, GROUP), bf16),
            pltpu.VMEM((OWN, TOTAL, HD), bf16),
            pltpu.VMEM((OWN, TOTAL, 2 * HD), bf16),
            pltpu.VMEM((OWN, TOTAL, HD), bf16),
            pltpu.VMEM((OWN, SIDE, 8, HD), jnp.float32),
            pltpu.VMEM((OWN, SIDE - 1, CHUNK, HD), bf16),
            pltpu.VMEM((OWN, SIDE - 1, 8, HD), jnp.float32),
            pltpu.VMEM((OWN, TOTAL, HD), bf16),
            pltpu.VMEM((OWN, SIDE, TOK, HD), bf16),
            pltpu.VMEM((SIDE * SIDE + 1, ROWS, HD), bf16),
        ]
        + [sems((SIDE,))] * 4
        + [sems((OWN, SIDE))] * 12,
        compiler_params=pltpu.CompilerParams(
            collective_id=0, has_side_effects=True, vmem_limit_bytes=48 * 2**20
        ),
        name="edit_attention",
    )(active_blocks, queries, keys, values)


def solution(mesh):
    placed = (P(("req", "seq"), None), P(("req", "seq"), None), P(("req", "seq"), None), P("req"))
    return jax.shard_map(
        local, mesh=mesh, in_specs=placed, out_specs=P(("req", "seq"), None), check_vma=False
    )
```

```python
import jax
import jax.numpy as jnp
from jax import lax
from jax.experimental import pallas as pl
from jax.experimental.pallas import tpu as pltpu
from jax.sharding import PartitionSpec as P

HEADS = 20
HD = 128
BLK = 128
BPD = 2
SIDE = 4
GROUP = SIDE * SIDE
OWN = HEADS // SIDE
ROWS = 64
PIECE = ROWS // SIDE
TOK = 256
CHUNK = GROUP * PIECE
WIDTH = OWN * HD
SCALE = HD ** -0.5 * 1.4426950408889634
MESH = pl.DeviceIdType.MESH
OTHERS = (1, 3, 2)
REACHED = [(i // SIDE, i % SIDE) for i in range(1, GROUP)]
BF16 = jnp.bfloat16


def attend_head(h, qbuf, kbuf, vbuf, obuf, lbuf, eye, top):
    columns = pl.ds(pl.multiple_of(h * HD, HD), HD)
    for part in range(SIDE):
        scores = lax.dot_general(
            qbuf[part, :, :, columns].reshape(CHUNK, HD), kbuf[h], (((1,), (1,)), ((), ())),
            preferred_element_type=jnp.float32,
        )
        high = jnp.max(scores, axis=-1, keepdims=True)
        weights = jnp.exp2((scores - high) * SCALE).astype(BF16)
        summed = jnp.dot(weights, vbuf[h], preferred_element_type=jnp.float32)
        totals = summed[:, HD:]
        obuf[h, part] = (summed[:, :HD] / totals).astype(BF16)
        logs = high * SCALE + jnp.log2(totals)
        first = jnp.sum(jnp.where(eye, logs[:BLK], 0.0), axis=0, keepdims=True)
        second = jnp.sum(jnp.where(eye, logs[BLK:], 0.0), axis=0, keepdims=True)
        lbuf[h, part] = jnp.where(top, first, second)


def merge_head(h, mine, obuf, lbuf, orecv, lrecv, pick):
    logs = [lbuf[h, mine]] + [lrecv[h, i] for i in range(SIDE - 1)]
    highest = jnp.maximum(jnp.maximum(logs[0], logs[1]), jnp.maximum(logs[2], logs[3]))
    factors = [jnp.exp2(one - highest) for one in logs]
    inverse = 1.0 / (factors[0] + factors[1] + factors[2] + factors[3])
    for half in range(2):
        rows = slice(half * BLK, (half + 1) * BLK)
        total = None
        for i in range(SIDE):
            share = factors[i] * inverse
            spread = jnp.broadcast_to(share[half : half + 1, :], (BLK, HD)).T
            piece = obuf[h, mine, rows, :] if i == 0 else orecv[h, i - 1, rows, :]
            term = spread * piece.astype(jnp.float32)
            total = term if total is None else total + term
        spots = GROUP // 2
        pick[half * spots : (half + 1) * spots] = total.astype(BF16).reshape(spots, PIECE, HD)


def kernel(
    act, q, k, v, out,
    qbuf, kbuf, vbuf, obuf, lbuf, orecv, lrecv, pick, stage,
    q_own, q1s, q1r, q2s, q2r, own, ks, kr, vs, vr, os, orr, ls, lr, d_own, ds, dr,
):
    core = lax.axis_index("req") % 2
    here = lax.axis_index("seq")
    x, y = here // SIDE, here % SIDE
    a = x + core * (y - x)
    b = y + core * (x - y)

    def device(da, db):
        ta, tb = (a + da) % SIDE, (b + db) % SIDE
        tx, ty = ta + core * (tb - ta), tb + core * (ta - tb)
        return tx * SIDE + ty

    def remote(src, dst, send, recv, da, db):
        return pltpu.make_async_remote_copy(
            src_ref=src, dst_ref=dst, send_sem=send, recv_sem=recv,
            device_id={"seq": device(da, db)}, device_id_type=MESH,
        )

    def arrived(ref, send, recv):
        return remote(ref, ref, send, recv, 1, 0)

    def head_columns(da, h):
        return pl.ds(pl.multiple_of(((a + da) % SIDE * OWN + h) * HD, HD), HD)

    query_parts = ((0, HD), (HD, WIDTH - HD))

    def query_columns(da, n):
        start, size = query_parts[n]
        return pl.ds(pl.multiple_of((a + da) % SIDE * WIDTH + start, HD), size)

    def query_first(n, i):
        start, size = query_parts[n]
        source = q.at[:, :, query_columns(i, n)]
        target = qbuf.at[:, b * SIDE + i, :, pl.ds(start, size)]
        if i == 0:
            return pltpu.make_async_copy(source, target, q_own.at[n])
        return remote(source, target, q1s.at[n, i], q1r.at[n, i], i, 0)

    def query_second(n, i):
        start, size = query_parts[n]
        part = qbuf.at[:, pl.ds(b * SIDE, SIDE), :, pl.ds(start, size)]
        return remote(part, part, q2s.at[n, i], q2r.at[n, i], 0, i)

    def key_copy(h, i):
        source = k.at[:, head_columns(i, h)]
        target = kbuf.at[h, pl.ds(i * TOK, TOK)]
        if i == 0:
            return pltpu.make_async_copy(source, target, own.at[h, 0])
        return remote(source, target, ks.at[h], kr.at[h], i, 0)

    def value_copy(h, i):
        source = v.at[:, head_columns(i, h)]
        target = vbuf.at[h, pl.ds(i * TOK, TOK), pl.ds(0, HD)]
        if i == 0:
            return pltpu.make_async_copy(source, target, own.at[h, 1])
        return remote(source, target, vs.at[h], vr.at[h], i, 0)

    def partial_copy(h, i):
        return remote(obuf.at[h, (b + i) % SIDE], orecv.at[h, i - 1], os.at[h], orr.at[h], 0, i)

    def log_copy(h, i):
        return remote(lbuf.at[h, (b + i) % SIDE], lrecv.at[h, i - 1], ls.at[h], lr.at[h], 0, i)

    def finished_copy(h, n):
        target = out.at[:, b, :, head_columns(0, h)]
        if n == 0:
            return pltpu.make_async_copy(stage.at[h, 0], target, d_own.at[h])
        da, db = REACHED[n - 1]
        return remote(stage.at[h, n], target, ds.at[h], dr.at[h], da, db)

    barrier = pltpu.get_barrier_semaphore()
    for da, db in REACHED:
        pl.semaphore_signal(barrier, inc=1, device_id={"seq": device(da, db)}, device_id_type=MESH)
    pl.semaphore_wait(barrier, len(REACHED))

    def send_head(h):
        for i in OTHERS + (0,):
            key_copy(h, i).start()
        for i in OTHERS + (0,):
            value_copy(h, i).start()

    for i in OTHERS + (0,):
        query_first(0, i).start()
    send_head(0)
    for i in OTHERS + (0,):
        query_first(1, i).start()

    @pl.loop(1, OWN)
    def _(h):
        send_head(h)

    @pl.loop(0, OWN)
    def _(h):
        vbuf[h, :, HD:] = jnp.ones((SIDE * TOK, HD), BF16)

    for n in range(2):
        for i in OTHERS + (0,):
            query_first(n, i).wait()
        for i in OTHERS:
            query_second(n, i).start()

    pick[GROUP] = jnp.zeros((PIECE, HD), BF16)
    places = []
    for owner in range(GROUP):
        ox, oy = owner // SIDE, owner % SIDE
        oa, ob = ox + core * (oy - ox), oy + core * (ox - oy)
        places.append(ob * SIDE + (a - oa + SIDE) % SIDE)
    sources = []
    for n in range(GROUP):
        block = device(n // SIDE, n % SIDE) * BPD
        for slot in range(BPD):
            spots = [jnp.int32(GROUP)] * 2
            for j in range(GROUP // 2):
                match = act[j] == block + slot
                spots = [jnp.where(match, places[2 * j + half], spots[half]) for half in range(2)]
            sources += spots

    line = lax.broadcasted_iota(jnp.int32, (BLK, HD), 0)
    eye = line == lax.broadcasted_iota(jnp.int32, (BLK, HD), 1)
    top = lax.broadcasted_iota(jnp.int32, (8, HD), 0) == 0
    for i in OTHERS:
        query_second(0, i).wait()

    @pl.loop(0, OWN + 1)
    def _(t):
        @pl.when(t == 1)
        def _():
            for i in OTHERS:
                query_second(1, i).wait()

        @pl.when(t < OWN)
        def _():
            key_copy(t, 0).wait()
            value_copy(t, 0).wait()
            arrived(kbuf.at[t, pl.ds(TOK, 3 * TOK)], ks.at[t], kr.at[t]).wait()
            arrived(vbuf.at[t, pl.ds(TOK, 3 * TOK), pl.ds(0, HD)], vs.at[t], vr.at[t]).wait()
            attend_head(t, qbuf, kbuf, vbuf, obuf, lbuf, eye, top)
            for i in OTHERS:
                partial_copy(t, i).start()
                log_copy(t, i).start()

        @pl.when(t >= 1)
        def _():
            h = t - 1
            arrived(orecv.at[h], os.at[h], orr.at[h]).wait()
            arrived(lrecv.at[h], ls.at[h], lr.at[h]).wait()
            merge_head(h, b, obuf, lbuf, orecv, lrecv, pick)
            for n in range(GROUP):
                for piece in range(2 * BPD):
                    stage[h, n, piece] = pick[sources[2 * BPD * n + piece]]
                finished_copy(h, n).start()

    @pl.loop(0, OWN)
    def _(h):
        finished_copy(h, 0).wait()
        arrived(stage.at[h, pl.ds(1, GROUP - 1)], ds.at[h], dr.at[h]).wait()


def local(queries, keys, values, active_blocks):
    sems = pltpu.SemaphoreType.DMA
    width = HEADS * HD
    edited = pl.pallas_call(
        kernel,
        out_shape=jax.ShapeDtypeStruct((2 * BPD, SIDE, PIECE, width), BF16),
        in_specs=[pl.BlockSpec(memory_space=pltpu.SMEM)] + [pl.BlockSpec(memory_space=pl.ANY)] * 3,
        out_specs=pl.BlockSpec(memory_space=pl.ANY),
        scratch_shapes=[
            pltpu.VMEM((SIDE, GROUP, PIECE, WIDTH), BF16),
            pltpu.VMEM((OWN, SIDE * TOK, HD), BF16),
            pltpu.VMEM((OWN, SIDE * TOK, 2 * HD), BF16),
            pltpu.VMEM((OWN, SIDE, CHUNK, HD), BF16),
            pltpu.VMEM((OWN, SIDE, 8, HD), jnp.float32),
            pltpu.VMEM((OWN, SIDE - 1, CHUNK, HD), BF16),
            pltpu.VMEM((OWN, SIDE - 1, 8, HD), jnp.float32),
            pltpu.VMEM((GROUP + 1, PIECE, HD), BF16),
            pltpu.VMEM((OWN, GROUP, 2 * BPD, PIECE, HD), BF16),
        ]
        + [sems((2,))]
        + [sems((2, SIDE))] * 4
        + [sems((OWN, 2))]
        + [sems((OWN,))] * 11,
        compiler_params=pltpu.CompilerParams(
            collective_id=0, has_side_effects=True, vmem_limit_bytes=62 * 2**20
        ),
        name="edit_attention",
    )(active_blocks, queries.reshape(SIDE, PIECE, width), keys, values)
    return edited.reshape(TOK, width)


def solution(mesh):
    placed = (P(("req", "seq"), None), P(("req", "seq"), None), P(("req", "seq"), None), P("req"))
    return jax.shard_map(
        local, mesh=mesh, in_specs=placed, out_specs=P(("req", "seq"), None), check_vma=False
    )
```

```python
import jax
import jax.numpy as jnp
from jax import lax
from jax.experimental import pallas as pl
from jax.experimental.pallas import tpu as pltpu
from jax.sharding import PartitionSpec as P

HEADS = 20
HD = 128
BLK = 128
BPD = 2
SIDE = 4
GROUP = SIDE * SIDE
OWN = HEADS // SIDE
ROWS = 64
PIECE = ROWS // SIDE
TOK = 256
CHUNK = GROUP * PIECE
WIDTH = OWN * HD
SCALE = HD ** -0.5 * 1.4426950408889634
MESH = pl.DeviceIdType.MESH
OTHERS = (1, 3, 2)
LAG = 3
REACHED = [(i // SIDE, i % SIDE) for i in range(1, GROUP)]
BF16 = jnp.bfloat16


def attend_head(h, qbuf, kbuf, vbuf, obuf, lbuf, eye, top):
    columns = pl.ds(pl.multiple_of(h * HD, HD), HD)
    for part in range(SIDE):
        scores = lax.dot_general(
            qbuf[part, :, :, columns].reshape(CHUNK, HD), kbuf[h], (((1,), (1,)), ((), ())),
            preferred_element_type=jnp.float32,
        )
        high = jnp.max(scores, axis=-1, keepdims=True)
        weights = jnp.exp2((scores - high) * SCALE).astype(BF16)
        summed = jnp.dot(weights, vbuf[h], preferred_element_type=jnp.float32)
        totals = summed[:, HD:]
        obuf[h, part] = (summed[:, :HD] / totals).astype(BF16)
        logs = high * SCALE + jnp.log2(totals)
        first = jnp.sum(jnp.where(eye, logs[:BLK], 0.0), axis=0, keepdims=True)
        second = jnp.sum(jnp.where(eye, logs[BLK:], 0.0), axis=0, keepdims=True)
        lbuf[h, part] = jnp.where(top, first, second)


def merge_head(h, mine, obuf, lbuf, orecv, lrecv, pick):
    logs = [lbuf[h, mine]] + [lrecv[h, i] for i in range(SIDE - 1)]
    highest = jnp.maximum(jnp.maximum(logs[0], logs[1]), jnp.maximum(logs[2], logs[3]))
    factors = [jnp.exp2(one - highest) for one in logs]
    inverse = 1.0 / (factors[0] + factors[1] + factors[2] + factors[3])
    for half in range(2):
        rows = slice(half * BLK, (half + 1) * BLK)
        total = None
        for i in range(SIDE):
            share = factors[i] * inverse
            spread = jnp.broadcast_to(share[half : half + 1, :], (BLK, HD)).T
            piece = obuf[h, mine, rows, :] if i == 0 else orecv[h, i - 1, rows, :]
            term = spread * piece.astype(jnp.float32)
            total = term if total is None else total + term
        spots = GROUP // 2
        pick[half * spots : (half + 1) * spots] = total.astype(BF16).reshape(spots, PIECE, HD)


def kernel(
    act, q, k, v, out,
    qbuf, kbuf, vbuf, obuf, lbuf, orecv, lrecv, pick, stage,
    q_own, q1s, q1r, q2s, q2r, own, ks, kr, vs, vr, os, orr, ls, lr, d_own, ds, dr,
):
    core = 1 - lax.axis_index("req") % 2
    here = lax.axis_index("seq")
    x, y = here // SIDE, here % SIDE
    a = x + core * (y - x)
    b = y + core * (x - y)

    def device(da, db):
        ta, tb = (a + da) % SIDE, (b + db) % SIDE
        tx, ty = ta + core * (tb - ta), tb + core * (ta - tb)
        return tx * SIDE + ty

    def remote(src, dst, send, recv, da, db):
        return pltpu.make_async_remote_copy(
            src_ref=src, dst_ref=dst, send_sem=send, recv_sem=recv,
            device_id={"seq": device(da, db)}, device_id_type=MESH,
        )

    def arrived(ref, send, recv):
        return remote(ref, ref, send, recv, 1, 0)

    def head_columns(da, h):
        return pl.ds(pl.multiple_of(((a + da) % SIDE * OWN + h) * HD, HD), HD)

    query_parts = ((0, HD), (HD, WIDTH - HD))

    def query_columns(da, n):
        start, size = query_parts[n]
        return pl.ds(pl.multiple_of((a + da) % SIDE * WIDTH + start, HD), size)

    def query_first(n, i):
        start, size = query_parts[n]
        source = q.at[:, :, query_columns(i, n)]
        target = qbuf.at[:, b * SIDE + i, :, pl.ds(start, size)]
        if i == 0:
            return pltpu.make_async_copy(source, target, q_own.at[n])
        return remote(source, target, q1s.at[n, i], q1r.at[n, i], i, 0)

    def query_second(n, i):
        start, size = query_parts[n]
        part = qbuf.at[:, pl.ds(b * SIDE, SIDE), :, pl.ds(start, size)]
        return remote(part, part, q2s.at[n, i], q2r.at[n, i], 0, i)

    def key_copy(h, i):
        source = k.at[:, head_columns(i, h)]
        target = kbuf.at[h, pl.ds(i * TOK, TOK)]
        if i == 0:
            return pltpu.make_async_copy(source, target, own.at[h, 0])
        return remote(source, target, ks.at[h], kr.at[h], i, 0)

    def value_copy(h, i):
        source = v.at[:, head_columns(i, h)]
        target = vbuf.at[h, pl.ds(i * TOK, TOK), pl.ds(0, HD)]
        if i == 0:
            return pltpu.make_async_copy(source, target, own.at[h, 1])
        return remote(source, target, vs.at[h], vr.at[h], i, 0)

    def partial_copy(h, i):
        return remote(obuf.at[h, (b + i) % SIDE], orecv.at[h, i - 1], os.at[h], orr.at[h], 0, i)

    def log_copy(h, i):
        return remote(lbuf.at[h, (b + i) % SIDE], lrecv.at[h, i - 1], ls.at[h], lr.at[h], 0, i)

    def finished_copy(h, n):
        target = out.at[:, b, :, head_columns(0, h)]
        if n == 0:
            return pltpu.make_async_copy(stage.at[h, 0], target, d_own.at[h])
        da, db = REACHED[n - 1]
        return remote(stage.at[h, n], target, ds.at[h], dr.at[h], da, db)

    barrier = pltpu.get_barrier_semaphore()
    for da, db in REACHED:
        pl.semaphore_signal(barrier, inc=1, device_id={"seq": device(da, db)}, device_id_type=MESH)
    pl.semaphore_wait(barrier, len(REACHED))

    def send_head(h):
        for i in OTHERS + (0,):
            key_copy(h, i).start()
        for i in OTHERS + (0,):
            value_copy(h, i).start()

    for i in OTHERS + (0,):
        query_first(0, i).start()
    send_head(0)
    for i in OTHERS + (0,):
        query_first(1, i).start()

    @pl.loop(1, OWN)
    def _(h):
        send_head(h)

    @pl.loop(0, OWN)
    def _(h):
        vbuf[h, :, HD:] = jnp.ones((SIDE * TOK, HD), BF16)

    for n in range(2):
        for i in OTHERS + (0,):
            query_first(n, i).wait()
        for i in OTHERS:
            query_second(n, i).start()

    pick[GROUP] = jnp.zeros((PIECE, HD), BF16)
    places = []
    for owner in range(GROUP):
        ox, oy = owner // SIDE, owner % SIDE
        oa, ob = ox + core * (oy - ox), oy + core * (ox - oy)
        places.append(ob * SIDE + (a - oa + SIDE) % SIDE)
    sources = []
    for n in range(GROUP):
        block = device(n // SIDE, n % SIDE) * BPD
        for slot in range(BPD):
            spots = [jnp.int32(GROUP)] * 2
            for j in range(GROUP // 2):
                match = act[j] == block + slot
                spots = [jnp.where(match, places[2 * j + half], spots[half]) for half in range(2)]
            sources += spots

    line = lax.broadcasted_iota(jnp.int32, (BLK, HD), 0)
    eye = line == lax.broadcasted_iota(jnp.int32, (BLK, HD), 1)
    top = lax.broadcasted_iota(jnp.int32, (8, HD), 0) == 0
    for i in OTHERS:
        query_second(0, i).wait()

    @pl.loop(0, OWN + LAG)
    def _(t):
        @pl.when(t == 1)
        def _():
            for i in OTHERS:
                query_second(1, i).wait()

        @pl.when(t < OWN)
        def _():
            key_copy(t, 0).wait()
            value_copy(t, 0).wait()
            arrived(kbuf.at[t, pl.ds(TOK, 3 * TOK)], ks.at[t], kr.at[t]).wait()
            arrived(vbuf.at[t, pl.ds(TOK, 3 * TOK), pl.ds(0, HD)], vs.at[t], vr.at[t]).wait()
            attend_head(t, qbuf, kbuf, vbuf, obuf, lbuf, eye, top)
            for i in OTHERS:
                partial_copy(t, i).start()
                log_copy(t, i).start()

        @pl.when(t >= LAG)
        def _():
            h = t - LAG
            arrived(orecv.at[h], os.at[h], orr.at[h]).wait()
            arrived(lrecv.at[h], ls.at[h], lr.at[h]).wait()
            merge_head(h, b, obuf, lbuf, orecv, lrecv, pick)
            for n in range(GROUP):
                for piece in range(2 * BPD):
                    stage[h, n, piece] = pick[sources[2 * BPD * n + piece]]
                finished_copy(h, n).start()

    @pl.loop(0, OWN)
    def _(h):
        finished_copy(h, 0).wait()
        arrived(stage.at[h, pl.ds(1, GROUP - 1)], ds.at[h], dr.at[h]).wait()


def local(queries, keys, values, active_blocks):
    sems = pltpu.SemaphoreType.DMA
    width = HEADS * HD
    edited = pl.pallas_call(
        kernel,
        out_shape=pltpu.VMEM((2 * BPD, SIDE, PIECE, width), BF16),
        in_specs=[pl.BlockSpec(memory_space=pltpu.SMEM)] + [pl.BlockSpec(memory_space=pl.ANY)] * 3,
        out_specs=pl.BlockSpec(memory_space=pl.ANY),
        scratch_shapes=[
            pltpu.VMEM((SIDE, GROUP, PIECE, WIDTH), BF16),
            pltpu.VMEM((OWN, SIDE * TOK, HD), BF16),
            pltpu.VMEM((OWN, SIDE * TOK, 2 * HD), BF16),
            pltpu.VMEM((OWN, SIDE, CHUNK, HD), BF16),
            pltpu.VMEM((OWN, SIDE, 8, HD), jnp.float32),
            pltpu.VMEM((OWN, SIDE - 1, CHUNK, HD), BF16),
            pltpu.VMEM((OWN, SIDE - 1, 8, HD), jnp.float32),
            pltpu.VMEM((GROUP + 1, PIECE, HD), BF16),
            pltpu.VMEM((OWN, GROUP, 2 * BPD, PIECE, HD), BF16),
        ]
        + [sems((2,))]
        + [sems((2, SIDE))] * 4
        + [sems((OWN, 2))]
        + [sems((OWN,))] * 11,
        compiler_params=pltpu.CompilerParams(
            collective_id=0, has_side_effects=True, vmem_limit_bytes=62 * 2**20
        ),
        name="edit_attention",
    )(active_blocks, queries.reshape(SIDE, PIECE, width), keys, values)
    return edited.reshape(TOK, width)


def solution(mesh):
    placed = (P(("req", "seq"), None), P(("req", "seq"), None), P(("req", "seq"), None), P("req"))
    return jax.shard_map(
        local, mesh=mesh, in_specs=placed, out_specs=P(("req", "seq"), None), check_vma=False
    )
```

```python
import jax
import jax.numpy as jnp
from jax import lax
from jax.experimental import pallas as pl
from jax.experimental.pallas import tpu as pltpu
from jax.sharding import PartitionSpec as P

HEADS = 20
HD = 128
BLK = 128
BPD = 2
SIDE = 4
GROUP = SIDE * SIDE
OWN = HEADS // SIDE
ROWS = 64
PIECE = ROWS // SIDE
TOK = 256
CHUNK = GROUP * PIECE
WIDTH = OWN * HD
SCALE = HD ** -0.5 * 1.4426950408889634
MESH = pl.DeviceIdType.MESH
OTHERS = (2, 1, 3)
FARTHEST_FIRST = (10, 6, 9, 14, 11, 5, 15, 7, 13, 2, 8, 1, 4, 3, 12, 0)
REACHED = [(i // SIDE, i % SIDE) for i in range(1, GROUP)]
BF16 = jnp.bfloat16


def attend_head(h, qbuf, kbuf, vbuf, obuf, lbuf, eye, top):
    columns = pl.ds(pl.multiple_of(h * HD, HD), HD)
    for part in range(SIDE):
        scores = lax.dot_general(
            qbuf[part, :, :, columns].reshape(CHUNK, HD), kbuf[h], (((1,), (1,)), ((), ())),
            preferred_element_type=jnp.float32,
        )
        high = jnp.max(scores, axis=-1, keepdims=True)
        weights = jnp.exp2((scores - high) * SCALE).astype(BF16)
        summed = jnp.dot(weights, vbuf[h], preferred_element_type=jnp.float32)
        totals = summed[:, HD:]
        obuf[h, part] = (summed[:, :HD] / totals).astype(BF16)
        logs = high * SCALE + jnp.log2(totals)
        first = jnp.sum(jnp.where(eye, logs[:BLK], 0.0), axis=0, keepdims=True)
        second = jnp.sum(jnp.where(eye, logs[BLK:], 0.0), axis=0, keepdims=True)
        lbuf[h, part] = jnp.where(top, first, second)


def merge_head(h, mine, obuf, lbuf, orecv, lrecv, pick):
    logs = [lbuf[h, mine]] + [lrecv[h, i] for i in range(SIDE - 1)]
    highest = jnp.maximum(jnp.maximum(logs[0], logs[1]), jnp.maximum(logs[2], logs[3]))
    factors = [jnp.exp2(one - highest) for one in logs]
    inverse = 1.0 / (factors[0] + factors[1] + factors[2] + factors[3])
    for half in range(2):
        rows = slice(half * BLK, (half + 1) * BLK)
        total = None
        for i in range(SIDE):
            share = factors[i] * inverse
            spread = jnp.broadcast_to(share[half : half + 1, :], (BLK, HD)).T
            piece = obuf[h, mine, rows, :] if i == 0 else orecv[h, i - 1, rows, :]
            term = spread * piece.astype(jnp.float32)
            total = term if total is None else total + term
        spots = GROUP // 2
        pick[half * spots : (half + 1) * spots] = total.astype(BF16).reshape(spots, PIECE, HD)


def kernel(
    act, q, k, v, out,
    qbuf, kbuf, vbuf, obuf, lbuf, orecv, lrecv, pick, stage,
    q_own, q1s, q1r, q2s, q2r, own, ks, kr, vs, vr, os, orr, ls, lr, d_own, ds, dr,
):
    core = 1 - lax.axis_index("req") % 2
    here = lax.axis_index("seq")
    x, y = here // SIDE, here % SIDE
    a = x + core * (y - x)
    b = y + core * (x - y)

    def device(da, db):
        ta, tb = (a + da) % SIDE, (b + db) % SIDE
        tx, ty = ta + core * (tb - ta), tb + core * (ta - tb)
        return tx * SIDE + ty

    def remote(src, dst, send, recv, da, db):
        return pltpu.make_async_remote_copy(
            src_ref=src, dst_ref=dst, send_sem=send, recv_sem=recv,
            device_id={"seq": device(da, db)}, device_id_type=MESH,
        )

    def arrived(ref, send, recv):
        return remote(ref, ref, send, recv, 1, 0)

    def head_columns(da, h):
        return pl.ds(pl.multiple_of(((a + da) % SIDE * OWN + h) * HD, HD), HD)

    query_parts = ((0, HD), (HD, WIDTH - HD))

    def query_columns(da, n):
        start, size = query_parts[n]
        return pl.ds(pl.multiple_of((a + da) % SIDE * WIDTH + start, HD), size)

    def query_first(n, i):
        start, size = query_parts[n]
        source = q.at[:, :, query_columns(i, n)]
        target = qbuf.at[:, b * SIDE + i, :, pl.ds(start, size)]
        if i == 0:
            return pltpu.make_async_copy(source, target, q_own.at[n])
        return remote(source, target, q1s.at[n, i], q1r.at[n, i], i, 0)

    def query_second(n, i):
        start, size = query_parts[n]
        part = qbuf.at[:, pl.ds(b * SIDE, SIDE), :, pl.ds(start, size)]
        return remote(part, part, q2s.at[n, i], q2r.at[n, i], 0, i)

    def key_copy(h, i):
        source = k.at[:, head_columns(i, h)]
        target = kbuf.at[h, pl.ds(i * TOK, TOK)]
        if i == 0:
            return pltpu.make_async_copy(source, target, own.at[h, 0])
        return remote(source, target, ks.at[h], kr.at[h], i, 0)

    def value_copy(h, i):
        source = v.at[:, head_columns(i, h)]
        target = vbuf.at[h, pl.ds(i * TOK, TOK), pl.ds(0, HD)]
        if i == 0:
            return pltpu.make_async_copy(source, target, own.at[h, 1])
        return remote(source, target, vs.at[h], vr.at[h], i, 0)

    def partial_copy(h, i):
        return remote(obuf.at[h, (b + i) % SIDE], orecv.at[h, i - 1], os.at[h], orr.at[h], 0, i)

    def log_copy(h, i):
        return remote(lbuf.at[h, (b + i) % SIDE], lrecv.at[h, i - 1], ls.at[h], lr.at[h], 0, i)

    def finished_copy(h, n):
        target = out.at[:, b, :, head_columns(0, h)]
        if n == 0:
            return pltpu.make_async_copy(stage.at[h, 0], target, d_own.at[h])
        da, db = REACHED[n - 1]
        return remote(stage.at[h, n], target, ds.at[h], dr.at[h], da, db)

    barrier = pltpu.get_barrier_semaphore()
    for da, db in REACHED:
        pl.semaphore_signal(barrier, inc=1, device_id={"seq": device(da, db)}, device_id_type=MESH)
    pl.semaphore_wait(barrier, len(REACHED))

    def send_head(h):
        for i in OTHERS + (0,):
            key_copy(h, i).start()
        for i in OTHERS + (0,):
            value_copy(h, i).start()

    for i in OTHERS + (0,):
        query_first(0, i).start()
    send_head(0)
    for i in OTHERS + (0,):
        query_first(1, i).start()

    @pl.loop(1, OWN)
    def _(h):
        send_head(h)

    @pl.loop(0, OWN)
    def _(h):
        vbuf[h, :, HD:] = jnp.ones((SIDE * TOK, HD), BF16)

    for n in range(2):
        for i in OTHERS + (0,):
            query_first(n, i).wait()
        for i in OTHERS:
            query_second(n, i).start()

    pick[GROUP] = jnp.zeros((PIECE, HD), BF16)
    places = []
    for owner in range(GROUP):
        ox, oy = owner // SIDE, owner % SIDE
        oa, ob = ox + core * (oy - ox), oy + core * (ox - oy)
        places.append(ob * SIDE + (a - oa + SIDE) % SIDE)
    sources = []
    for n in range(GROUP):
        block = device(n // SIDE, n % SIDE) * BPD
        for slot in range(BPD):
            spots = [jnp.int32(GROUP)] * 2
            for j in range(GROUP // 2):
                match = act[j] == block + slot
                spots = [jnp.where(match, places[2 * j + half], spots[half]) for half in range(2)]
            sources += spots

    line = lax.broadcasted_iota(jnp.int32, (BLK, HD), 0)
    eye = line == lax.broadcasted_iota(jnp.int32, (BLK, HD), 1)
    top = lax.broadcasted_iota(jnp.int32, (8, HD), 0) == 0
    for i in OTHERS:
        query_second(0, i).wait()

    lag = 2 + core

    @pl.loop(0, OWN + 3)
    def _(t):
        @pl.when(t == 1)
        def _():
            for i in OTHERS:
                query_second(1, i).wait()

        @pl.when(t < OWN)
        def _():
            key_copy(t, 0).wait()
            value_copy(t, 0).wait()
            arrived(kbuf.at[t, pl.ds(TOK, 3 * TOK)], ks.at[t], kr.at[t]).wait()
            arrived(vbuf.at[t, pl.ds(TOK, 3 * TOK), pl.ds(0, HD)], vs.at[t], vr.at[t]).wait()
            attend_head(t, qbuf, kbuf, vbuf, obuf, lbuf, eye, top)
            for i in OTHERS:
                partial_copy(t, i).start()
                log_copy(t, i).start()

        @pl.when((t >= lag) & (t < OWN + lag))
        def _():
            h = t - lag
            arrived(orecv.at[h], os.at[h], orr.at[h]).wait()
            arrived(lrecv.at[h], ls.at[h], lr.at[h]).wait()
            merge_head(h, b, obuf, lbuf, orecv, lrecv, pick)
            for n in FARTHEST_FIRST:
                for piece in range(2 * BPD):
                    stage[h, n, piece] = pick[sources[2 * BPD * n + piece]]
                finished_copy(h, n).start()

    @pl.loop(0, OWN)
    def _(h):
        finished_copy(h, 0).wait()
        arrived(stage.at[h, pl.ds(1, GROUP - 1)], ds.at[h], dr.at[h]).wait()


def local(queries, keys, values, active_blocks):
    sems = pltpu.SemaphoreType.DMA
    width = HEADS * HD
    edited = pl.pallas_call(
        kernel,
        out_shape=pltpu.VMEM((2 * BPD, SIDE, PIECE, width), BF16),
        in_specs=[pl.BlockSpec(memory_space=pltpu.SMEM)] + [pl.BlockSpec(memory_space=pl.ANY)] * 3,
        out_specs=pl.BlockSpec(memory_space=pl.ANY),
        scratch_shapes=[
            pltpu.VMEM((SIDE, GROUP, PIECE, WIDTH), BF16),
            pltpu.VMEM((OWN, SIDE * TOK, HD), BF16),
            pltpu.VMEM((OWN, SIDE * TOK, 2 * HD), BF16),
            pltpu.VMEM((OWN, SIDE, CHUNK, HD), BF16),
            pltpu.VMEM((OWN, SIDE, 8, HD), jnp.float32),
            pltpu.VMEM((OWN, SIDE - 1, CHUNK, HD), BF16),
            pltpu.VMEM((OWN, SIDE - 1, 8, HD), jnp.float32),
            pltpu.VMEM((GROUP + 1, PIECE, HD), BF16),
            pltpu.VMEM((OWN, GROUP, 2 * BPD, PIECE, HD), BF16),
        ]
        + [sems((2,))]
        + [sems((2, SIDE))] * 4
        + [sems((OWN, 2))]
        + [sems((OWN,))] * 11,
        compiler_params=pltpu.CompilerParams(
            collective_id=0, has_side_effects=True, vmem_limit_bytes=62 * 2**20
        ),
        name="edit_attention",
    )(active_blocks, queries.reshape(SIDE, PIECE, width), keys, values)
    return edited.reshape(TOK, width)


def solution(mesh):
    placed = (P(("req", "seq"), None), P(("req", "seq"), None), P(("req", "seq"), None), P("req"))
    return jax.shard_map(
        local, mesh=mesh, in_specs=placed, out_specs=P(("req", "seq"), None), check_vma=False
    )
```

```python
import jax
import jax.numpy as jnp
from jax import lax
from jax.experimental import pallas as pl
from jax.experimental.pallas import tpu as pltpu
from jax.sharding import PartitionSpec as P

HEADS = 20
HD = 128
BLK = 128
BPD = 2
SIDE = 4
GROUP = SIDE * SIDE
OWN = HEADS // SIDE
ROWS = 64
PIECE = ROWS // SIDE
TOK = 256
CHUNK = GROUP * PIECE
WIDTH = OWN * HD
SCALE = HD ** -0.5 * 1.4426950408889634
MESH = pl.DeviceIdType.MESH
OTHERS = (2, 1, 3)
FARTHEST_FIRST = (10, 6, 9, 14, 11, 5, 15, 7, 13, 2, 8, 1, 4, 3, 12, 0)
REACHED = [(i // SIDE, i % SIDE) for i in range(1, GROUP)]
BF16 = jnp.bfloat16


def attend_head(h, qbuf, kbuf, vbuf, obuf, lbuf, eye, top):
    columns = pl.ds(pl.multiple_of(h * HD, HD), HD)
    for part in range(SIDE):
        scores = lax.dot_general(
            qbuf[part, :, :, columns].reshape(CHUNK, HD), kbuf[h], (((1,), (1,)), ((), ())),
            preferred_element_type=jnp.float32,
        )
        high = jnp.max(scores, axis=-1, keepdims=True)
        weights = jnp.exp2((scores - high) * SCALE).astype(BF16)
        summed = jnp.dot(weights, vbuf[h], preferred_element_type=jnp.float32)
        totals = summed[:, HD:]
        obuf[h, part] = (summed[:, :HD] / totals).astype(BF16)
        logs = high * SCALE + jnp.log2(totals)
        first = jnp.sum(jnp.where(eye, logs[:BLK], 0.0), axis=0, keepdims=True)
        second = jnp.sum(jnp.where(eye, logs[BLK:], 0.0), axis=0, keepdims=True)
        lbuf[h, part] = jnp.where(top, first, second)


def merge_head(h, mine, obuf, lbuf, orecv, lrecv, pick):
    logs = [lbuf[h, mine]] + [lrecv[h, i] for i in range(SIDE - 1)]
    highest = jnp.maximum(jnp.maximum(logs[0], logs[1]), jnp.maximum(logs[2], logs[3]))
    factors = [jnp.exp2(one - highest) for one in logs]
    inverse = 1.0 / (factors[0] + factors[1] + factors[2] + factors[3])
    for half in range(2):
        rows = slice(half * BLK, (half + 1) * BLK)
        total = None
        for i in range(SIDE):
            share = factors[i] * inverse
            spread = jnp.broadcast_to(share[half : half + 1, :], (BLK, HD)).T
            piece = obuf[h, mine, rows, :] if i == 0 else orecv[h, i - 1, rows, :]
            term = spread * piece.astype(jnp.float32)
            total = term if total is None else total + term
        spots = GROUP // 2
        pick[half * spots : (half + 1) * spots] = total.astype(BF16).reshape(spots, PIECE, HD)


def kernel(
    act, q, k, v, out,
    qbuf, kbuf, vbuf, obuf, lbuf, orecv, lrecv, pick, stage,
    q_own, q1s, q1r, q2s, q2r, own, ks, kr, vs, vr, os, orr, ls, lr, d_own, ds, dr,
):
    core = 1 - lax.axis_index("req") % 2
    here = lax.axis_index("seq")
    x, y = here // SIDE, here % SIDE
    a = x + core * (y - x)
    b = y + core * (x - y)

    def device(da, db):
        ta, tb = (a + da) % SIDE, (b + db) % SIDE
        tx, ty = ta + core * (tb - ta), tb + core * (ta - tb)
        return tx * SIDE + ty

    def remote(src, dst, send, recv, da, db):
        return pltpu.make_async_remote_copy(
            src_ref=src, dst_ref=dst, send_sem=send, recv_sem=recv,
            device_id={"seq": device(da, db)}, device_id_type=MESH,
        )

    def arrived(ref, send, recv):
        return remote(ref, ref, send, recv, 1, 0)

    def head_columns(da, h):
        return pl.ds(pl.multiple_of(((a + da) % SIDE * OWN + h) * HD, HD), HD)

    query_parts = ((0, HD), (HD, WIDTH - HD))

    def query_columns(da, n):
        start, size = query_parts[n]
        return pl.ds(pl.multiple_of((a + da) % SIDE * WIDTH + start, HD), size)

    def query_first(n, i):
        start, size = query_parts[n]
        source = q.at[:, :, query_columns(i, n)]
        target = qbuf.at[:, b * SIDE + i, :, pl.ds(start, size)]
        if i == 0:
            return pltpu.make_async_copy(source, target, q_own.at[n])
        return remote(source, target, q1s.at[n, i], q1r.at[n, i], i, 0)

    def query_second(n, i):
        start, size = query_parts[n]
        part = qbuf.at[:, pl.ds(b * SIDE, SIDE), :, pl.ds(start, size)]
        return remote(part, part, q2s.at[n, i], q2r.at[n, i], 0, i)

    def key_copy(h, i):
        source = k.at[:, head_columns(i, h)]
        target = kbuf.at[h, pl.ds(i * TOK, TOK)]
        if i == 0:
            return pltpu.make_async_copy(source, target, own.at[h, 0])
        return remote(source, target, ks.at[h], kr.at[h], i, 0)

    def value_copy(h, i):
        source = v.at[:, head_columns(i, h)]
        target = vbuf.at[h, pl.ds(i * TOK, TOK), pl.ds(0, HD)]
        if i == 0:
            return pltpu.make_async_copy(source, target, own.at[h, 1])
        return remote(source, target, vs.at[h], vr.at[h], i, 0)

    def partial_copy(h, i):
        return remote(obuf.at[h, (b + i) % SIDE], orecv.at[h, i - 1], os.at[h], orr.at[h], 0, i)

    def log_copy(h, i):
        return remote(lbuf.at[h, (b + i) % SIDE], lrecv.at[h, i - 1], ls.at[h], lr.at[h], 0, i)

    def finished_copy(h, n):
        target = out.at[:, b, :, head_columns(0, h)]
        if n == 0:
            return pltpu.make_async_copy(stage.at[h, 0], target, d_own.at[h])
        da, db = REACHED[n - 1]
        return remote(stage.at[h, n], target, ds.at[h], dr.at[h], da, db)

    barrier = pltpu.get_barrier_semaphore()
    for da, db in REACHED:
        pl.semaphore_signal(barrier, inc=1, device_id={"seq": device(da, db)}, device_id_type=MESH)
    pl.semaphore_wait(barrier, len(REACHED))

    def send_head(h):
        for i in OTHERS + (0,):
            key_copy(h, i).start()
        for i in OTHERS + (0,):
            value_copy(h, i).start()

    for i in OTHERS + (0,):
        query_first(0, i).start()
    send_head(0)
    for i in OTHERS + (0,):
        query_first(1, i).start()

    for n in range(2):
        for i in OTHERS + (0,):
            query_first(n, i).wait()
        for i in OTHERS:
            query_second(n, i).start()
        if n == 0:

            @pl.loop(1, OWN)
            def _(h):
                send_head(h)

            @pl.loop(0, OWN)
            def _(h):
                vbuf[h, :, HD:] = jnp.ones((SIDE * TOK, HD), BF16)

    pick[GROUP] = jnp.zeros((PIECE, HD), BF16)
    places = []
    for owner in range(GROUP):
        ox, oy = owner // SIDE, owner % SIDE
        oa, ob = ox + core * (oy - ox), oy + core * (ox - oy)
        places.append(ob * SIDE + (a - oa + SIDE) % SIDE)
    sources = []
    for n in range(GROUP):
        block = device(n // SIDE, n % SIDE) * BPD
        for slot in range(BPD):
            spots = [jnp.int32(GROUP)] * 2
            for j in range(GROUP // 2):
                match = act[j] == block + slot
                spots = [jnp.where(match, places[2 * j + half], spots[half]) for half in range(2)]
            sources += spots

    line = lax.broadcasted_iota(jnp.int32, (BLK, HD), 0)
    eye = line == lax.broadcasted_iota(jnp.int32, (BLK, HD), 1)
    top = lax.broadcasted_iota(jnp.int32, (8, HD), 0) == 0
    for i in OTHERS:
        query_second(0, i).wait()

    lag = 2

    @pl.loop(0, OWN + 3)
    def _(t):
        @pl.when(t == 1)
        def _():
            for i in OTHERS:
                query_second(1, i).wait()

        @pl.when(t < OWN)
        def _():
            key_copy(t, 0).wait()
            value_copy(t, 0).wait()
            arrived(kbuf.at[t, pl.ds(TOK, 3 * TOK)], ks.at[t], kr.at[t]).wait()
            arrived(vbuf.at[t, pl.ds(TOK, 3 * TOK), pl.ds(0, HD)], vs.at[t], vr.at[t]).wait()
            attend_head(t, qbuf, kbuf, vbuf, obuf, lbuf, eye, top)
            for i in OTHERS:
                partial_copy(t, i).start()
                log_copy(t, i).start()

        @pl.when((t >= lag) & (t < OWN + lag))
        def _():
            h = t - lag
            arrived(orecv.at[h], os.at[h], orr.at[h]).wait()
            arrived(lrecv.at[h], ls.at[h], lr.at[h]).wait()
            merge_head(h, b, obuf, lbuf, orecv, lrecv, pick)
            for n in FARTHEST_FIRST:
                for piece in range(2 * BPD):
                    stage[h, n, piece] = pick[sources[2 * BPD * n + piece]]
                finished_copy(h, n).start()

    @pl.loop(0, OWN)
    def _(h):
        finished_copy(h, 0).wait()
        arrived(stage.at[h, pl.ds(1, GROUP - 1)], ds.at[h], dr.at[h]).wait()


def local(queries, keys, values, active_blocks):
    sems = pltpu.SemaphoreType.DMA
    width = HEADS * HD
    edited = pl.pallas_call(
        kernel,
        out_shape=pltpu.VMEM((2 * BPD, SIDE, PIECE, width), BF16),
        in_specs=[pl.BlockSpec(memory_space=pltpu.SMEM)] + [pl.BlockSpec(memory_space=pl.ANY)] * 3,
        out_specs=pl.BlockSpec(memory_space=pl.ANY),
        scratch_shapes=[
            pltpu.VMEM((SIDE, GROUP, PIECE, WIDTH), BF16),
            pltpu.VMEM((OWN, SIDE * TOK, HD), BF16),
            pltpu.VMEM((OWN, SIDE * TOK, 2 * HD), BF16),
            pltpu.VMEM((OWN, SIDE, CHUNK, HD), BF16),
            pltpu.VMEM((OWN, SIDE, 8, HD), jnp.float32),
            pltpu.VMEM((OWN, SIDE - 1, CHUNK, HD), BF16),
            pltpu.VMEM((OWN, SIDE - 1, 8, HD), jnp.float32),
            pltpu.VMEM((GROUP + 1, PIECE, HD), BF16),
            pltpu.VMEM((OWN, GROUP, 2 * BPD, PIECE, HD), BF16),
        ]
        + [sems((2,))]
        + [sems((2, SIDE))] * 4
        + [sems((OWN, 2))]
        + [sems((OWN,))] * 11,
        compiler_params=pltpu.CompilerParams(
            collective_id=0, has_side_effects=True, vmem_limit_bytes=62 * 2**20
        ),
        name="edit_attention",
    )(active_blocks, queries.reshape(SIDE, PIECE, width), keys, values)
    return edited.reshape(TOK, width)


def solution(mesh):
    placed = (P(("req", "seq"), None), P(("req", "seq"), None), P(("req", "seq"), None), P("req"))
    return jax.shard_map(
        local, mesh=mesh, in_specs=placed, out_specs=P(("req", "seq"), None), check_vma=False
    )
```

```python
import jax
import jax.numpy as jnp
from jax import lax
from jax.experimental import pallas as pl
from jax.experimental.pallas import tpu as pltpu
from jax.sharding import PartitionSpec as P

HEADS = 20
HD = 128
BLK = 128
BPD = 2
SIDE = 4
GROUP = SIDE * SIDE
OWN = HEADS // SIDE
ROWS = 64
PIECE = ROWS // SIDE
TOK = 256
CHUNK = GROUP * PIECE
WIDTH = OWN * HD
SCALE = HD ** -0.5 * 1.4426950408889634
MESH = pl.DeviceIdType.MESH
OTHERS = (2, 1, 3)
FARTHEST_FIRST = (10, 6, 9, 14, 11, 5, 15, 7, 13, 2, 8, 1, 4, 3, 12, 0)
REACHED = [(i // SIDE, i % SIDE) for i in range(1, GROUP)]
BF16 = jnp.bfloat16


def attend_head(h, qbuf, kbuf, vbuf, obuf, lbuf, eye, top):
    columns = pl.ds(pl.multiple_of(h * HD, HD), HD)
    for part in range(SIDE):
        scores = lax.dot_general(
            qbuf[part, :, :, columns].reshape(CHUNK, HD), kbuf[h], (((1,), (1,)), ((), ())),
            preferred_element_type=jnp.float32,
        )
        high = jnp.max(scores, axis=-1, keepdims=True)
        weights = jnp.exp2((scores - high) * SCALE).astype(BF16)
        summed = jnp.dot(weights, vbuf[h], preferred_element_type=jnp.float32)
        totals = summed[:, HD:]
        obuf[h, part] = (summed[:, :HD] / totals).astype(BF16)
        packed = []
        for rows in (slice(0, BLK), slice(BLK, CHUNK)):
            most = jnp.sum(jnp.where(eye, high[rows], 0.0), axis=0, keepdims=True)
            count = jnp.sum(jnp.where(eye, totals[rows], 0.0), axis=0, keepdims=True)
            packed.append(most * SCALE + jnp.log2(count))
        first, second = packed
        lbuf[h, part] = jnp.where(top, first, second)


def merge_head(h, mine, obuf, lbuf, orecv, lrecv, pick):
    logs = [lbuf[h, mine]] + [lrecv[h, i] for i in range(SIDE - 1)]
    highest = jnp.maximum(jnp.maximum(logs[0], logs[1]), jnp.maximum(logs[2], logs[3]))
    factors = [jnp.exp2(one - highest) for one in logs]
    inverse = 1.0 / (factors[0] + factors[1] + factors[2] + factors[3])
    for half in range(2):
        rows = slice(half * BLK, (half + 1) * BLK)
        total = None
        for i in range(SIDE):
            share = factors[i] * inverse
            spread = jnp.broadcast_to(share[half : half + 1, :], (BLK, HD)).T
            piece = obuf[h, mine, rows, :] if i == 0 else orecv[h, i - 1, rows, :]
            term = spread * piece.astype(jnp.float32)
            total = term if total is None else total + term
        spots = GROUP // 2
        pick[half * spots : (half + 1) * spots] = total.astype(BF16).reshape(spots, PIECE, HD)


def kernel(
    act, q, k, v, out,
    qbuf, kbuf, vbuf, obuf, lbuf, orecv, lrecv, pick, stage,
    q_own, q1s, q1r, q2s, q2r, own, ks, kr, vs, vr, os, orr, ls, lr, d_own, ds, dr,
):
    core = 1 - lax.axis_index("req") % 2
    here = lax.axis_index("seq")
    x, y = here // SIDE, here % SIDE
    a = x + core * (y - x)
    b = y + core * (x - y)

    def device(da, db):
        ta, tb = (a + da) % SIDE, (b + db) % SIDE
        tx, ty = ta + core * (tb - ta), tb + core * (ta - tb)
        return tx * SIDE + ty

    def remote(src, dst, send, recv, da, db):
        return pltpu.make_async_remote_copy(
            src_ref=src, dst_ref=dst, send_sem=send, recv_sem=recv,
            device_id={"seq": device(da, db)}, device_id_type=MESH,
        )

    def arrived(ref, send, recv):
        return remote(ref, ref, send, recv, 1, 0)

    def head_columns(da, h):
        return pl.ds(pl.multiple_of(((a + da) % SIDE * OWN + h) * HD, HD), HD)

    query_parts = ((0, HD), (HD, WIDTH - HD))

    def query_columns(da, n):
        start, size = query_parts[n]
        return pl.ds(pl.multiple_of((a + da) % SIDE * WIDTH + start, HD), size)

    def query_first(n, i):
        start, size = query_parts[n]
        source = q.at[:, :, query_columns(i, n)]
        target = qbuf.at[:, b * SIDE + i, :, pl.ds(start, size)]
        if i == 0:
            return pltpu.make_async_copy(source, target, q_own.at[n])
        return remote(source, target, q1s.at[n, i], q1r.at[n, i], i, 0)

    def query_second(n, i):
        start, size = query_parts[n]
        part = qbuf.at[:, pl.ds(b * SIDE, SIDE), :, pl.ds(start, size)]
        return remote(part, part, q2s.at[n, i], q2r.at[n, i], 0, i)

    def key_copy(h, i):
        source = k.at[:, head_columns(i, h)]
        target = kbuf.at[h, pl.ds(i * TOK, TOK)]
        if i == 0:
            return pltpu.make_async_copy(source, target, own.at[h, 0])
        return remote(source, target, ks.at[h], kr.at[h], i, 0)

    def value_copy(h, i):
        source = v.at[:, head_columns(i, h)]
        target = vbuf.at[h, pl.ds(i * TOK, TOK), pl.ds(0, HD)]
        if i == 0:
            return pltpu.make_async_copy(source, target, own.at[h, 1])
        return remote(source, target, vs.at[h], vr.at[h], i, 0)

    def partial_copy(h, i):
        return remote(obuf.at[h, (b + i) % SIDE], orecv.at[h, i - 1], os.at[h], orr.at[h], 0, i)

    def log_copy(h, i):
        return remote(lbuf.at[h, (b + i) % SIDE], lrecv.at[h, i - 1], ls.at[h], lr.at[h], 0, i)

    def finished_copy(h, n):
        target = out.at[:, b, :, head_columns(0, h)]
        if n == 0:
            return pltpu.make_async_copy(stage.at[h, 0], target, d_own.at[h])
        da, db = REACHED[n - 1]
        return remote(stage.at[h, n], target, ds.at[h], dr.at[h], da, db)

    barrier = pltpu.get_barrier_semaphore()
    for da, db in REACHED:
        pl.semaphore_signal(barrier, inc=1, device_id={"seq": device(da, db)}, device_id_type=MESH)
    pl.semaphore_wait(barrier, len(REACHED))

    def send_head(h):
        for i in OTHERS + (0,):
            key_copy(h, i).start()
        for i in OTHERS + (0,):
            value_copy(h, i).start()

    for i in OTHERS + (0,):
        query_first(0, i).start()
    send_head(0)
    for i in OTHERS + (0,):
        query_first(1, i).start()

    for n in range(2):
        for i in OTHERS + (0,):
            query_first(n, i).wait()
        for i in OTHERS:
            query_second(n, i).start()
        if n == 0:

            @pl.loop(1, OWN)
            def _(h):
                send_head(h)

            @pl.loop(0, OWN)
            def _(h):
                vbuf[h, :, HD:] = jnp.ones((SIDE * TOK, HD), BF16)

    pick[GROUP] = jnp.zeros((PIECE, HD), BF16)
    places = []
    for owner in range(GROUP):
        ox, oy = owner // SIDE, owner % SIDE
        oa, ob = ox + core * (oy - ox), oy + core * (ox - oy)
        places.append(ob * SIDE + (a - oa + SIDE) % SIDE)
    sources = []
    for n in range(GROUP):
        block = device(n // SIDE, n % SIDE) * BPD
        for slot in range(BPD):
            spots = [jnp.int32(GROUP)] * 2
            for j in range(GROUP // 2):
                match = act[j] == block + slot
                spots = [jnp.where(match, places[2 * j + half], spots[half]) for half in range(2)]
            sources += spots

    line = lax.broadcasted_iota(jnp.int32, (BLK, HD), 0)
    eye = line == lax.broadcasted_iota(jnp.int32, (BLK, HD), 1)
    top = lax.broadcasted_iota(jnp.int32, (8, HD), 0) == 0
    for i in OTHERS:
        query_second(0, i).wait()

    lag = 2

    @pl.loop(0, OWN + 3)
    def _(t):
        @pl.when(t == 1)
        def _():
            for i in OTHERS:
                query_second(1, i).wait()

        @pl.when(t < OWN)
        def _():
            key_copy(t, 0).wait()
            value_copy(t, 0).wait()
            arrived(kbuf.at[t, pl.ds(TOK, 3 * TOK)], ks.at[t], kr.at[t]).wait()
            arrived(vbuf.at[t, pl.ds(TOK, 3 * TOK), pl.ds(0, HD)], vs.at[t], vr.at[t]).wait()
            attend_head(t, qbuf, kbuf, vbuf, obuf, lbuf, eye, top)
            for i in OTHERS:
                partial_copy(t, i).start()
                log_copy(t, i).start()

        @pl.when((t >= lag) & (t < OWN + lag))
        def _():
            h = t - lag
            arrived(orecv.at[h], os.at[h], orr.at[h]).wait()
            arrived(lrecv.at[h], ls.at[h], lr.at[h]).wait()
            merge_head(h, b, obuf, lbuf, orecv, lrecv, pick)
            for n in FARTHEST_FIRST:
                for piece in range(2 * BPD):
                    stage[h, n, piece] = pick[sources[2 * BPD * n + piece]]
                finished_copy(h, n).start()

    @pl.loop(0, OWN)
    def _(h):
        finished_copy(h, 0).wait()
        arrived(stage.at[h, pl.ds(1, GROUP - 1)], ds.at[h], dr.at[h]).wait()


def local(queries, keys, values, active_blocks):
    sems = pltpu.SemaphoreType.DMA
    width = HEADS * HD
    edited = pl.pallas_call(
        kernel,
        out_shape=pltpu.VMEM((2 * BPD, SIDE, PIECE, width), BF16),
        in_specs=[pl.BlockSpec(memory_space=pltpu.SMEM)] + [pl.BlockSpec(memory_space=pl.ANY)] * 3,
        out_specs=pl.BlockSpec(memory_space=pl.ANY),
        scratch_shapes=[
            pltpu.VMEM((SIDE, GROUP, PIECE, WIDTH), BF16),
            pltpu.VMEM((OWN, SIDE * TOK, HD), BF16),
            pltpu.VMEM((OWN, SIDE * TOK, 2 * HD), BF16),
            pltpu.VMEM((OWN, SIDE, CHUNK, HD), BF16),
            pltpu.VMEM((OWN, SIDE, 8, HD), jnp.float32),
            pltpu.VMEM((OWN, SIDE - 1, CHUNK, HD), BF16),
            pltpu.VMEM((OWN, SIDE - 1, 8, HD), jnp.float32),
            pltpu.VMEM((GROUP + 1, PIECE, HD), BF16),
            pltpu.VMEM((OWN, GROUP, 2 * BPD, PIECE, HD), BF16),
        ]
        + [sems((2,))]
        + [sems((2, SIDE))] * 4
        + [sems((OWN, 2))]
        + [sems((OWN,))] * 11,
        compiler_params=pltpu.CompilerParams(
            collective_id=0, has_side_effects=True, vmem_limit_bytes=62 * 2**20
        ),
        name="edit_attention",
    )(active_blocks, queries.reshape(SIDE, PIECE, width), keys, values)
    return edited.reshape(TOK, width)


def solution(mesh):
    placed = (P(("req", "seq"), None), P(("req", "seq"), None), P(("req", "seq"), None), P("req"))
    return jax.shard_map(
        local, mesh=mesh, in_specs=placed, out_specs=P(("req", "seq"), None), check_vma=False
    )
```
